256 devices in a mesh: dp: 16 (over z, core), ctx: 16 (over y, x).
Axes of the slice: x: 4, y: 4, z: 8, core: 2. Of those that a mesh axis runs over, the one named last changes fastest.
Arguments:
- corpus: bfloat16 [4096, 3584], P('dp'), may hold values from -60 to 60
- owners: int32 [16, 2048, 1], P('dp', 'ctx'), may hold values from 0 to 15; in each aligned block of 128 rows (0 to 127, 128 to 255, ..., all dimensions but the last counted through in order) at most 16 rows name the same one
- local_rows: int32 [16, 2048], P('dp', 'ctx'), may hold values from 0 to 255
- doc_ids: int32 [16, 2048], P('dp'), may hold values from 0 to 15, never falling along the last dimension, each value on 1 to 512 neighbouring positions
- norm_gain: float32 [3584], replicated, may hold values from 0.1 to 1.9
- wqkv: bfloat16 [3584, 3072], P('dp'), may hold values from -3 to 3
- qkv_bias: float32 [3072], replicated, may hold values from -3 to 3
Outputs:
- context: bfloat16 [16, 2048, 2048], P('dp', 'ctx')
The draws below stay inside these ranges and needn't reach their ends.
Inputs may be any that keep to these rules, and one draw needn't show every extreme that they name: `owners`: among the 128 positions of one device, at most 16 name one owner, a bound that some block reaches. `doc_ids`: document numbers never fall along a window; a document holds at most 512 positions, and one holds exactly that many.
All inputs are finite; a program needn't handle non-finite values.
Results may differ from the reference program's by a relative error of at most 0.0045.
The reference program's roundings to bfloat16 on the way (of `fetched`, `normed` and `weights`) count: a program that leaves them out, or rounds other values in their place, can miss the bound.
Values may be sent and summed in bfloat16 or wider, within the bound.
A program may use at most 128 MiB of HBM per device.

```python
import math
import jax
import jax.numpy as jnp
import numpy as np
from jax import lax

D = 3584
KEY_VALUE_HEADS = 4
HEAD_SIZE = 128
QUERY_HEADS = 16
TOK_DEV = 128
SEQ = 2048
CORP_DEV = 256
CAP = 16
QKV = 3072
N_DP = 16
N_CTX = 16


def draw_corpus(key, part):
    key = jax.random.fold_in(key, 11)
    base_key, scale_key = jax.random.split(key, 2)
    row_count = N_DP * CORP_DEV
    row_scale = jnp.exp(jax.random.uniform(scale_key, (row_count, 1), jnp.float32, 0.0, math.log(10.0)))
    base = jnp.clip(jax.random.normal(base_key, (row_count, D), jnp.float32), -6.0, 6.0)
    return (base * row_scale).astype(jnp.bfloat16)


def draw_wqkv(key, part):
    key = jax.random.fold_in(key, 23)
    base_key = jax.random.fold_in(key, 0)
    base = jnp.clip(jax.random.normal(base_key, (D, QKV), jnp.float32), -6.0, 6.0)
    return (base / math.sqrt(D)).astype(jnp.bfloat16)


def place_ends(drawn, stream_key, low, high):
    extent = drawn.shape
    spot = [jax.random.randint(jax.random.fold_in(stream_key, axis), (), 0, extent[axis]) for axis in range(len(extent))]
    drawn = drawn.at[tuple(spot)].set(low)
    longest = extent.index(max(extent))
    spot[longest] = (spot[longest] + 1) % extent[longest]
    return drawn.at[tuple(spot)].set(high)


def split_up(count, total, most, skew):
    weights = [(1 << 20) // math.isqrt(rank ** skew) + 1 for rank in range(2, count + 1)]
    rest, holding = total - most - (count - 1), [1] * (count - 1)
    while rest > 0:
        candidates = [i for i in range(count - 1) if holding[i] < most]
        pool, budget = sum([weights[i] for i in candidates]), rest
        for i in candidates:
            addition = min(most - holding[i], max(1, budget * weights[i] // pool), rest)
            holding[i] = holding[i] + addition
            rest = rest - addition
    return np.array([most] + holding)


def ragged(stream_key, amount, total, reach, lean):
    if amount == 2:
        one = jax.random.randint(stream_key, (), max(1, total - reach), min(reach, total - 1) + 1)
        return jnp.stack([one, total - one])
    sizes = jnp.asarray(split_up(amount, total, reach, lean), jnp.int32)
    pairs = (amount - 1) // 2
    donor, taker = sizes[1:1 + 2 * pairs:2], sizes[2:2 + 2 * pairs:2]
    slack = jnp.minimum(donor - 1, reach - taker)
    passed = jax.random.randint(jax.random.fold_in(stream_key, 1), (pairs,), 0, 1 << 20) % (slack + 1)
    sizes = sizes.at[1:1 + 2 * pairs:2].set(donor - passed).at[2:2 + 2 * pairs:2].set(taker + passed)
    return sizes[jax.random.permutation(jax.random.fold_in(stream_key, 2), amount)]


def deal_out(stream_key, own, number, rows, count, top, bound, lean):
    sequence = jax.random.permutation(stream_key, count)
    crowded, ordinary = load_shares(count, rows * top, bound, lean, True), load_shares(count, rows * top, bound, lean, False)
    places = jnp.arange(count)

    def named(sizes, turn):
        used = int((sizes > 0).sum())
        fixed = max(1, used // 4)
        passed = fixed + (places - fixed + turn * (used - fixed)) % max(1, count - fixed)
        return jnp.zeros((count,), jnp.int32).at[sequence[jnp.where(places < fixed, places, passed)]].set(jnp.asarray(sizes, jnp.int32))

    sizes = jnp.where(number % 4 == 0, named(crowded, number // 4), named(ordinary, number - number // 4 - 1))
    mixed = jax.random.permutation(jax.random.fold_in(own, 3), count)
    donor, sink = mixed[0:count // 2 * 2:2], mixed[1:count // 2 * 2:2]
    room = jnp.minimum(sizes[donor] - 1, bound - sizes[sink]) // 2
    room = jnp.where((donor == sequence[0]) | (sink == sequence[0]) | (sizes[sink] == 0), 0, jnp.maximum(room, 0))
    passed = jax.random.randint(jax.random.fold_in(own, 4), (count // 2,), 0, 1 << 20) % (room + 1)
    sizes = sizes.at[donor].add(-passed).at[sink].add(passed)
    items = jnp.searchsorted(jnp.cumsum(sizes), jnp.arange(rows * top), side="right").astype(jnp.int32)
    listing = items.reshape(top, rows).T
    listing = listing[jax.random.permutation(jax.random.fold_in(own, 1), rows)]
    turn = jax.random.randint(jax.random.fold_in(own, 2), (rows, 1), 0, top)
    return jnp.take_along_axis(listing, (jnp.arange(top)[None, :] + turn) % top, axis=1)


def load_shares(count, total, bound, slope, full):
    weights = [(1 << 20) // math.isqrt(standing ** slope) + 1 for standing in range(1, count + 1)]
    largest = bound if full else min(bound, max(-(-total // count), total * weights[0] // sum(weights)))
    least = 1 if total - largest >= count - 1 else 0
    holding, surplus = [largest] + [least] * (count - 1), total - largest - least * (count - 1)
    while surplus > 0:
        candidates = [i for i in range(1, count) if holding[i] < largest] or [i for i in range(1, count) if holding[i] < bound]
        mass, left = sum([weights[i] for i in candidates]), surplus
        for i in candidates:
            more = min(bound - holding[i], max(1, left * weights[i] // mass), surplus)
            holding[i] = holding[i] + more
            surplus = surplus - more
    return np.array(holding)


def centred(stream_key, extent, scale, limit, kind=jnp.bfloat16):
    return jnp.clip(scale * jax.random.normal(stream_key, extent, jnp.float32), -limit, limit).astype(kind)


def setup_inputs(seed: int = 0) -> dict:
    streams_of = jax.random.split(jax.random.key(seed), 8)
    corpus = draw_corpus(jax.random.fold_in(streams_of[7], 71), 0)
    owners_keys = jax.random.split(jax.random.fold_in(streams_of[1], 1), N_DP * SEQ // TOK_DEV)
    owners_turns = jax.random.permutation(jax.random.fold_in(streams_of[1], 3), N_DP * SEQ // TOK_DEV)
    owners = jax.vmap(lambda own, number: deal_out(jax.random.fold_in(streams_of[1], 2), own, number, TOK_DEV, N_DP, 1, CAP, 2))(owners_keys, owners_turns).reshape((N_DP, SEQ, 1))
    local_rows = place_ends(jax.random.randint(streams_of[2], (N_DP, SEQ), 0, CORP_DEV), jax.random.fold_in(streams_of[2], 1), 0, CORP_DEV - 1).astype(jnp.int32)
    doc_ids = jax.vmap(lambda own: jnp.searchsorted(jnp.cumsum(ragged(own, N_CTX, SEQ, 4 * TOK_DEV, 2)), jnp.arange(SEQ), side="right"))(jax.random.split(streams_of[3], N_DP)).reshape((N_DP, SEQ)).astype(jnp.int32)
    norm_gain = jnp.clip(1.0 + 0.18 * jax.random.normal(streams_of[4], (D,), jnp.float32), 0.1, 1.9)
    wqkv = draw_wqkv(jax.random.fold_in(streams_of[7], 71), 0)
    qkv_bias = centred(streams_of[6], (QKV,), 0.5, 3.0, jnp.float32)
    return {"corpus": corpus, "owners": owners, "local_rows": local_rows, "doc_ids": doc_ids, "norm_gain": norm_gain, "wqkv": wqkv, "qkv_bias": qkv_bias}


EPS = 1e-06
ROPE_BASE = 1000000.0

def apply_rotary(tensor, token_positions):
    half_width = tensor.shape[-1] // 2
    frequency = ROPE_BASE ** (-jnp.arange(half_width, dtype=jnp.float32) * 2.0 / tensor.shape[-1])
    angles = token_positions.astype(jnp.float32)[:, None] * frequency[None, :]
    cosine = jnp.cos(angles)[:, None, :]
    sine_table = jnp.sin(angles)[:, None, :]
    leading = tensor[..., :half_width]
    trailing = tensor[..., half_width:]
    return jnp.concatenate([leading * cosine - trailing * sine_table, trailing * cosine + leading * sine_table], axis=-1)

def window_context(fetched, labels, norm_gain, wqkv, qkv_bias):
    floats = fetched.astype(jnp.float32)
    mean_square = lax.optimization_barrier(jnp.mean(floats * floats, axis=-1, keepdims=True))
    normed = (floats * lax.rsqrt(mean_square + EPS) * norm_gain).astype(jnp.bfloat16)
    projected_input = jnp.dot(normed, wqkv, preferred_element_type=jnp.float32) + qkv_bias
    token_length = normed.shape[0]
    token_positions = jnp.arange(token_length, dtype=jnp.int32)
    queries = apply_rotary(projected_input[:, :QUERY_HEADS * HEAD_SIZE].reshape(token_length, QUERY_HEADS, HEAD_SIZE), token_positions).astype(jnp.bfloat16)
    key_matrix = apply_rotary(projected_input[:, QUERY_HEADS * HEAD_SIZE:(QUERY_HEADS + KEY_VALUE_HEADS) * HEAD_SIZE].reshape(token_length, KEY_VALUE_HEADS, HEAD_SIZE), token_positions).astype(jnp.bfloat16)
    value_matrix = projected_input[:, (QUERY_HEADS + KEY_VALUE_HEADS) * HEAD_SIZE:].reshape(token_length, KEY_VALUE_HEADS, HEAD_SIZE).astype(jnp.bfloat16)
    queries, key_matrix, value_matrix = lax.optimization_barrier((queries, key_matrix, value_matrix))
    key_expanded = jnp.repeat(key_matrix, QUERY_HEADS // KEY_VALUE_HEADS, axis=1).astype(jnp.float32)
    value_expanded = jnp.repeat(value_matrix, QUERY_HEADS // KEY_VALUE_HEADS, axis=1).astype(jnp.float32)
    block_len = min(512, token_length)
    span = min(token_length, block_len + 4 * TOK_DEV)
    score_scale = HEAD_SIZE ** (-0.5)

    def one_block(number):
        offset = number * block_len
        key_start = jnp.clip(offset + block_len - span, 0, token_length - span).astype(jnp.int32)
        query_rows = lax.dynamic_slice_in_dim(queries, offset, block_len, 0).astype(jnp.float32)
        key_part = lax.dynamic_slice_in_dim(key_expanded, key_start, span, 0)
        value_part = lax.dynamic_slice_in_dim(value_expanded, key_start, span, 0)
        query_pos = offset + jnp.arange(block_len, dtype=jnp.int32)
        key_pos = key_start + jnp.arange(span, dtype=jnp.int32)
        query_lab = lax.dynamic_slice_in_dim(labels, offset, block_len, 0)
        key_lab = lax.dynamic_slice_in_dim(labels, key_start, span, 0)
        scores = jnp.einsum('qnd,knd->nqk', query_rows, key_part) * score_scale
        visible = (query_lab[:, None] == key_lab[None, :]) & (key_pos[None, :] <= query_pos[:, None])
        scores = jnp.where(visible[None], scores, -jnp.inf)
        highest = lax.optimization_barrier(jnp.max(scores, axis=2, keepdims=True))
        exponent = jnp.exp(scores - highest)
        running = lax.optimization_barrier(jnp.sum(exponent, axis=2))
        weights = lax.optimization_barrier(exponent.astype(jnp.bfloat16)).astype(jnp.float32)
        mixture = jnp.einsum('nqk,knd->qnd', weights, value_part)
        return (mixture / jnp.transpose(running)[:, :, None]).astype(jnp.bfloat16)
    blocks = lax.map(one_block, jnp.arange(token_length // block_len, dtype=jnp.int32))
    return blocks.reshape(token_length, QUERY_HEADS * HEAD_SIZE)

def reference(corpus, owners, local_rows, doc_ids, norm_gain, wqkv, qkv_bias):

    def window(inputs):
        owner_col, row_local, labels = inputs
        row_index = (owner_col[:, 0] * CORP_DEV + row_local).astype(jnp.int32)
        fetched = jnp.take(corpus, row_index, axis=0)
        return window_context(fetched, labels, norm_gain, wqkv, qkv_bias)
    return lax.map(window, (owners, local_rows, doc_ids))
```

```python
import functools

import jax
import jax.numpy as jnp
import numpy as np
from jax import lax
from jax.experimental import pallas as pl
from jax.experimental.pallas import tpu as pltpu
from jax.sharding import PartitionSpec as P

KEY_VALUE_HEADS = 4
HEAD_SIZE = 128
QUERY_HEADS = 16
GROUP = QUERY_HEADS // KEY_VALUE_HEADS
EPS = 1e-06
ROPE_BASE = 1000000.0
MESH = pl.DeviceIdType.MESH
BLOCK = 128
REACH = 512
LOG2E = 1.4426950408889634


def rotary_tables(length):
    half = HEAD_SIZE // 2
    frequency = (ROPE_BASE ** (-np.arange(half, dtype=np.float64) * 2.0 / HEAD_SIZE)).astype(np.float32)
    angles = (np.arange(length, dtype=np.float32)[:, None] * frequency[None, :]).astype(np.float64)
    cosine, sine = np.cos(angles), np.sin(angles)
    return (
        np.concatenate([cosine, cosine], axis=1).astype(np.float32),
        np.concatenate([-sine, sine], axis=1).astype(np.float32),
    )


def rotate(rows, cosine, sine):
    return rows * cosine + pltpu.roll(rows, HEAD_SIZE // 2, 1) * sine


def attend_kernel(
    n_ctx, index_ref, table_ref, labels_ref, cos_ref, sin_ref, out_ref,
    picked, query_buf, key_buf, value_buf, label_buf, block_buf, send_sem, recv_sem,
):
    dp = lax.axis_index("dp")
    me = lax.axis_index("ctx")
    length = index_ref.shape[0] * index_ref.shape[1]
    blocks = length // BLOCK
    pad = REACH

    barrier = pltpu.get_barrier_semaphore()

    def greet(step, carry):
        pl.semaphore_signal(barrier, inc=1, device_id=(dp, lax.rem(me + step, n_ctx)), device_id_type=MESH)
        return carry

    lax.fori_loop(1, n_ctx, greet, 0)

    unroll = 16

    def pick(block, carry):
        def some(part, inner):
            for u in range(unroll):
                row = part * unroll + u
                target = pl.multiple_of((block * BLOCK + row) * 4, 4)
                picked[pl.ds(target, 4), :] = table_ref[index_ref[block, row]]
            return inner

        return lax.fori_loop(0, BLOCK // unroll, some, carry)

    lax.fori_loop(0, blocks, pick, 0)

    key_buf[pl.ds(0, pad), :] = jnp.zeros((pad, HEAD_SIZE), jnp.bfloat16)
    value_buf[pl.ds(0, pad), :] = jnp.zeros((pad, HEAD_SIZE), jnp.bfloat16)
    label_buf[...] = jnp.full(label_buf.shape, -1, jnp.int32)
    for block in range(blocks):
        label_buf[pl.ds(pad // BLOCK + block, 1), 0, :] = labels_ref[:, pl.ds(block * BLOCK, BLOCK)]

    def turn(block, carry):
        start = pl.multiple_of(block * BLOCK, BLOCK)
        cosine = cos_ref[pl.ds(start, BLOCK), :]
        sine = sin_ref[pl.ds(start, BLOCK), :]
        base = pl.multiple_of(start * 4, BLOCK)
        query_buf[pl.ds(start, BLOCK), :] = rotate(
            picked[pl.ds(base, BLOCK, stride=4), :], cosine, sine
        ).astype(jnp.bfloat16)
        key_buf[pl.ds(pad + start, BLOCK), :] = rotate(
            picked[pl.ds(base + 1, BLOCK, stride=4), :], cosine, sine
        ).astype(jnp.bfloat16)
        value_buf[pl.ds(pad + start, BLOCK), :] = picked[pl.ds(base + 2, BLOCK, stride=4), :].astype(jnp.bfloat16)
        return carry

    lax.fori_loop(0, blocks, turn, 0)
    pl.semaphore_wait(barrier, n_ctx - 1)

    reach_blocks = pad // BLOCK
    causal = lax.broadcasted_iota(jnp.int32, (BLOCK, BLOCK), 1) <= lax.broadcasted_iota(
        jnp.int32, (BLOCK, BLOCK), 0
    )
    factor = HEAD_SIZE ** (-0.5) * LOG2E

    def one_block(block):
        start = pl.multiple_of(block * BLOCK, BLOCK)
        query = query_buf[pl.ds(start, BLOCK), :]
        keys = key_buf[pl.ds(start, pad + BLOCK), :]
        values = value_buf[pl.ds(start, pad + BLOCK), :]
        query_labels = jnp.transpose(
            jnp.broadcast_to(label_buf[block + reach_blocks], (BLOCK, BLOCK)).astype(jnp.float32)
        )
        scores = lax.dot_general(
            query, keys, (((1,), (1,)), ((), ())), preferred_element_type=jnp.float32
        )
        parts = []
        for number in range(reach_blocks + 1):
            part = scores[:, number * BLOCK : (number + 1) * BLOCK]
            key_labels = jnp.broadcast_to(label_buf[block + number], (BLOCK, BLOCK)).astype(jnp.float32)
            visible = key_labels == query_labels
            if number == reach_blocks:
                visible = visible & causal
            parts.append(jnp.where(visible, part, -jnp.inf))
        highest = functools.reduce(jnp.maximum, parts)
        highest = jnp.max(highest, axis=1, keepdims=True)
        exponents = [jnp.exp2((part - highest) * factor) for part in parts]
        total = jnp.sum(functools.reduce(jnp.add, exponents), axis=1, keepdims=True)
        weights = jnp.concatenate([e.astype(jnp.bfloat16) for e in exponents], axis=1)
        mixture = jnp.dot(weights, values, preferred_element_type=jnp.float32)
        return (mixture / total).astype(jnp.bfloat16)

    def block_copy(step):
        block = lax.rem(me + step, n_ctx)
        return pltpu.make_async_remote_copy(
            src_ref=block_buf.at[step],
            dst_ref=out_ref.at[:, pl.ds(pl.multiple_of(me * HEAD_SIZE, HEAD_SIZE), HEAD_SIZE)],
            send_sem=send_sem.at[step],
            recv_sem=recv_sem.at[step],
            device_id=(dp, block),
            device_id_type=MESH,
        )

    def work(step, carry):
        block_buf[step] = one_block(lax.rem(me + step, n_ctx))
        block_copy(step).start()
        return carry

    lax.fori_loop(1, n_ctx, work, 0)
    out_ref[:, pl.ds(pl.multiple_of(me * HEAD_SIZE, HEAD_SIZE), HEAD_SIZE)] = one_block(me)

    def finish(step, carry):
        block_copy(step).wait()
        return carry

    lax.fori_loop(1, n_ctx, finish, 0)


def attend(n_ctx, index, table, labels, cosine, sine):
    length = index.shape[0] * index.shape[1]
    vmem = pl.BlockSpec(memory_space=pltpu.VMEM)
    return pl.pallas_call(
        functools.partial(attend_kernel, n_ctx),
        out_shape=jax.ShapeDtypeStruct((length // n_ctx, QUERY_HEADS * HEAD_SIZE), jnp.bfloat16),
        in_specs=[pl.BlockSpec(memory_space=pltpu.SMEM), vmem, vmem, vmem, vmem],
        out_specs=vmem,
        scratch_shapes=[
            pltpu.VMEM((length * 4, HEAD_SIZE), jnp.float32),
            pltpu.VMEM((length, HEAD_SIZE), jnp.bfloat16),
            pltpu.VMEM((REACH + length, HEAD_SIZE), jnp.bfloat16),
            pltpu.VMEM((REACH + length, HEAD_SIZE), jnp.bfloat16),
            pltpu.VMEM(((REACH + length) // BLOCK, 1, BLOCK), jnp.int32),
            pltpu.VMEM((n_ctx, BLOCK, HEAD_SIZE), jnp.bfloat16),
            pltpu.SemaphoreType.DMA((n_ctx,)),
            pltpu.SemaphoreType.DMA((n_ctx,)),
        ],
        compiler_params=pltpu.CompilerParams(
            collective_id=0, has_side_effects=True, vmem_limit_bytes=48 * 1024 * 1024
        ),
    )(index, table, labels, cosine, sine)


def per_device(corpus, owners, local_rows, doc_ids, norm_gain, wqkv, qkv_bias):
    n_ctx = lax.axis_size("ctx")
    ctx = lax.axis_index("ctx")
    corpus_rows = corpus.shape[0]
    index = owners[0, :, 0] * corpus_rows + local_rows[0]
    index = lax.all_gather(index, "ctx", axis=0, tiled=False)
    floats = corpus.astype(jnp.float32)
    mean_square = jnp.mean(floats * floats, axis=-1, keepdims=True)
    normed = (floats * lax.rsqrt(mean_square + EPS) * norm_gain).astype(jnp.bfloat16)
    starts = [
        ctx * HEAD_SIZE,
        (QUERY_HEADS + ctx // GROUP) * HEAD_SIZE,
        (QUERY_HEADS + KEY_VALUE_HEADS + ctx // GROUP) * HEAD_SIZE,
    ]
    columns = jnp.concatenate([lax.dynamic_slice_in_dim(wqkv, s, HEAD_SIZE, 1) for s in starts], axis=1)
    bias = jnp.concatenate([lax.dynamic_slice_in_dim(qkv_bias, s, HEAD_SIZE, 0) for s in starts])
    columns = lax.all_gather(columns, "dp", axis=0, tiled=True)
    projected = jnp.dot(normed, columns, preferred_element_type=jnp.float32) + bias
    projected = lax.all_gather(projected, "dp", axis=0, tiled=True)
    table = jnp.pad(projected, ((0, 0), (0, HEAD_SIZE))).reshape(-1, 4, HEAD_SIZE)
    length = index.shape[0] * index.shape[1]
    cosine, sine = rotary_tables(length)
    return attend(n_ctx, index, table, doc_ids, jnp.asarray(cosine), jnp.asarray(sine))[None]


def solution(mesh):
    return jax.shard_map(
        per_device,
        mesh=mesh,
        in_specs=(
            P("dp", None),
            P("dp", "ctx", None),
            P("dp", "ctx"),
            P("dp", None),
            P(),
            P("dp", None),
            P(),
        ),
        out_specs=P("dp", "ctx", None),
        check_vma=False,
    )
```
